32 devices in a mesh: groups: 2 (over y), ctx: 4 (over z), mp: 4 (over x, core).
Axes of the slice: x: 2, y: 2, z: 4, core: 2. Of those that a mesh axis runs over, the one named last changes fastest.
Arguments:
- queries: bfloat16 [2048, 4096], P(('groups', 'ctx'), 'mp'), parts along dimension 0, may hold values from -18 to 18
- keyvals: bfloat16 [2048, 512], P(('groups', 'ctx', 'mp')), parts along dimension 0, may hold values from -6 to 6
- segment_ids: int32 [2048], P('groups'), parts along dimension 0, may hold values from 0 to 2, never falling along the last dimension, each value on 1 to 512 neighbouring positions
- residual: bfloat16 [2048, 4096], P(('groups', 'ctx', 'mp')), parts along dimension 0, may hold values from -180 to 180
- out_weight: bfloat16 [4096, 4096], P('mp', 'ctx'), may hold values from -0.375 to 0.375
- lru_weight: bfloat16 [4096, 4096], P('ctx', 'mp'), may hold values from -0.09375 to 0.09375
- conv_weight: float32 [4, 4096], P(None, 'mp'), may hold values from -3 to 3
- gate_decay_w: bfloat16 [16, 256, 256], P('mp'), may hold values from -0.375 to 0.375
- gate_input_w: bfloat16 [16, 256, 256], P('mp'), may hold values from -0.375 to 0.375
- gate_decay_b: float32 [4096], P('mp'), may hold values from -3 to 3
- gate_input_b: float32 [4096], P('mp'), may hold values from -3 to 3
- decay_codes: int32 [4096], P('mp'), may hold values from 0 to 15
- norm_gain: float32 [4096], replicated, may hold values from 0.1 to 1.9
Outputs:
- resid_out: bfloat16 [2048, 4096], P(('groups', 'ctx', 'mp')), parts along dimension 0
- lru_out: bfloat16 [2048, 4096], P(('groups', 'ctx'), 'mp'), parts along dimension 0
The draws below stay inside these ranges and needn't reach their ends.
There are 2 independent parts, one for each index of `groups`. The reference program is written for one: setup_inputs(seed, part) draws one part's arguments, and reference() takes and returns one part's arrays. A program takes and returns all parts, laid end to end along the dimension named above; an argument that names none is the same for every part. Nothing has to cross between parts.
All inputs are finite; a program needn't handle non-finite values.
Results may differ from the reference program's by a relative error of at most 0.017.
Values may be sent and summed in bfloat16 or wider, within the bound.
A program may use at most 64 MiB of HBM per device.

```python
import math
import jax
import jax.numpy as jnp
import numpy as np
from jax import lax

D = 4096
H = 16
HD = 256
WIN = 2048
LRU = 4096
NBLK = 16
CONV = 4
LEVELS = 16
BW = 256
TOKENS = 1024
N_MP = 4


def draw_queries(key, part):
    values = jnp.clip(2.0 * jax.random.normal(jax.random.fold_in(key, 3), (TOKENS, H * HD), jnp.float32), -8.0, 8.0)
    return values.astype(jnp.bfloat16)


def draw_keyvals(key, part):
    values = jnp.clip(jax.random.normal(jax.random.fold_in(key, 4), (TOKENS, 2 * HD), jnp.float32), -6.0, 6.0)
    return values.astype(jnp.bfloat16)


def draw_residual(key, part):
    values = jnp.clip(jax.random.normal(jax.random.fold_in(key, 5), (TOKENS, D), jnp.float32), -6.0, 6.0)
    return values.astype(jnp.bfloat16)


def touch_ends(array, rng, low, high):
    index_at = [jax.random.randint(jax.random.fold_in(rng, axis), (), 0, length) for axis, length in enumerate(array.shape)]
    longest = array.shape.index(max(array.shape))
    beside = index_at[:longest] + [(index_at[longest] + 1) % array.shape[longest]] + index_at[longest + 1:]
    return array.at[tuple(index_at)].set(low).at[tuple(beside)].set(high)


def level_of(key, extent, pieces, least, largest):
    def one(axis_at, blocks):
        draws = jax.random.uniform(jax.random.fold_in(jax.random.fold_in(key, 6), axis_at), (blocks,), jnp.float32, least / len(pieces), largest / len(pieces))
        return jnp.repeat(jnp.exp(draws), extent[axis_at] // blocks).reshape((-1,) + (1,) * (len(extent) - axis_at - 1))

    level = one(*pieces[0])
    for cut in pieces[1:]:
        level = level * one(*cut)
    return level


def split_up(number_of, total, most, lean):
    weights = [(1 << 20) // math.isqrt(rank ** lean) + 1 for rank in range(2, number_of + 1)]
    spare, counts = total - most - (number_of - 1), [1] * (number_of - 1)
    while spare > 0:
        movable = [i for i in range(number_of - 1) if counts[i] < most]
        mass, remaining = sum([weights[i] for i in movable]), spare
        for i in movable:
            extra = min(most - counts[i], max(1, remaining * weights[i] // mass), spare)
            counts[i] = counts[i] + extra
            spare = spare - extra
    return np.array([most] + counts)


def ragged(stream_key, number_of, total, limit, lean):
    if number_of == 2:
        one = jax.random.randint(stream_key, (), max(1, total - limit), min(limit, total - 1) + 1)
        return jnp.stack([one, total - one])
    tallies = jnp.asarray(split_up(number_of, total, limit, lean), jnp.int32)
    twos = (number_of - 1) // 2
    giver, receiver = tallies[1:1 + 2 * twos:2], tallies[2:2 + 2 * twos:2]
    room = jnp.minimum(giver - 1, limit - receiver)
    moved = jax.random.randint(jax.random.fold_in(stream_key, 1), (twos,), 0, 1 << 20) % (room + 1)
    tallies = tallies.at[1:1 + 2 * twos:2].set(giver - moved).at[2:2 + 2 * twos:2].set(receiver + moved)
    return tallies[jax.random.permutation(jax.random.fold_in(stream_key, 2), number_of)]


def noise(own_key, extent, scale, most, cuts=(), held_as=jnp.bfloat16):
    array = jax.random.normal(own_key, extent, jnp.float32) * scale
    if len(cuts) > 0:
        array = level_of(own_key, extent, cuts, -0.22, 0.18) * array
    return jnp.clip(array, min=-most, max=most).astype(held_as)


def setup_inputs(seed: int = 0, part: int = 0) -> dict:
    streams_of = jax.random.split(jax.random.key(seed), 14)
    part_keys = jax.random.split(jax.random.fold_in(streams_of[13], part), 14)
    queries = draw_queries(jax.random.fold_in(jax.random.fold_in(streams_of[13], part), 71), part)
    keyvals = draw_keyvals(jax.random.fold_in(jax.random.fold_in(streams_of[13], part), 71), part)
    segment_ids = jnp.searchsorted(jnp.cumsum(ragged(part_keys[2], 3, TOKENS, TOKENS // 2, 0)), jnp.arange(TOKENS), side="right").astype(jnp.int32)
    residual = draw_residual(jax.random.fold_in(jax.random.fold_in(streams_of[13], part), 71), part)
    out_weight = noise(streams_of[4], (H * HD, D), HD ** -0.5, 0.375, ((0, 4), (1, 4)))
    lru_weight = noise(streams_of[5], (D, LRU), D ** -0.5, 0.09375, ((0, 4), (1, 4)))
    conv_weight = noise(streams_of[6], (CONV, LRU), 0.5, 3.0, ((1, 4),), jnp.float32)
    gate_decay_w = noise(streams_of[7], (NBLK, BW, BW), BW ** -0.5, 0.375, ((0, 4),))
    gate_input_w = noise(streams_of[8], (NBLK, BW, BW), BW ** -0.5, 0.375, ((0, 4),))
    gate_decay_b = noise(streams_of[9], (LRU,), 1.0, 3.0, ((0, 4),), jnp.float32)
    gate_input_b = noise(streams_of[10], (LRU,), 1.0, 3.0, ((0, 4),), jnp.float32)
    decay_codes = touch_ends(jax.random.randint(streams_of[11], (LRU,), 0, LEVELS), jax.random.fold_in(streams_of[11], 1), 0, LEVELS - 1).astype(jnp.int32)
    norm_gain = jnp.clip(1.0 + 0.18 * jax.random.normal(streams_of[12], (D,), jnp.float32), 0.1, 1.9)
    return dict(queries=queries, keyvals=keyvals, segment_ids=segment_ids, residual=residual, out_weight=out_weight, lru_weight=lru_weight, conv_weight=conv_weight, gate_decay_w=gate_decay_w, gate_input_w=gate_input_w, gate_decay_b=gate_decay_b, gate_input_b=gate_input_b, decay_codes=decay_codes, norm_gain=norm_gain)


def decay_rates():
    levels = jnp.arange(LEVELS, dtype=jnp.float32)
    return 0.006 * jnp.exp(-levels * (math.log(3000.0) / (LEVELS - 1)))

def chain_link(former, latter):
    return (former[0] * latter[0], latter[0] * former[1] + latter[1])

def reference(queries, keyvals, segment_ids, residual, out_weight, lru_weight, conv_weight, gate_decay_w, gate_input_w, gate_decay_b, gate_input_b, decay_codes, norm_gain):
    block_rows = min(512, TOKENS)
    block_count = TOKENS // block_rows
    pad_kv = jnp.concatenate([jnp.zeros((WIN, 2 * HD), keyvals.dtype), keyvals], axis=0)
    pad_seg = jnp.concatenate([jnp.full((WIN,), -1, jnp.int32), segment_ids.astype(jnp.int32)])
    score_scale = 1.0 / math.sqrt(HD)

    def attend(block_index):
        first_row = (block_index * block_rows).astype(jnp.int32)
        query_block = lax.dynamic_slice_in_dim(queries, first_row, block_rows, 0).reshape(block_rows, H, HD)
        key_block = lax.dynamic_slice_in_dim(pad_kv, first_row, WIN + block_rows, 0)
        key_seg = lax.dynamic_slice_in_dim(pad_seg, first_row, WIN + block_rows, 0)
        query_seg = lax.dynamic_slice_in_dim(segment_ids.astype(jnp.int32), first_row, block_rows, 0)
        query_pos = first_row + jnp.arange(block_rows, dtype=jnp.int32)
        key_pos = first_row - WIN + jnp.arange(WIN + block_rows, dtype=jnp.int32)
        distance = query_pos[:, None] - key_pos[None, :]
        allowed = (distance >= 0) & (distance < WIN) & (query_seg[:, None] == key_seg[None, :])
        scores = jnp.einsum('thd,kd->htk', query_block.astype(jnp.float32), key_block[:, :HD].astype(jnp.float32)) * score_scale
        scores = jnp.where(allowed[None], scores, -1e+30)
        row_top = lax.optimization_barrier(jnp.max(scores, axis=-1, keepdims=True))
        weights = jnp.exp(scores - row_top)
        probs = (weights / lax.optimization_barrier(jnp.sum(weights, axis=-1, keepdims=True))).astype(jnp.bfloat16)
        gathered = jnp.einsum('htk,kd->thd', probs.astype(jnp.float32), key_block[:, HD:].astype(jnp.float32))
        return gathered.reshape(block_rows, H * HD).astype(jnp.bfloat16)
    attended = lax.map(attend, jnp.arange(block_count, dtype=jnp.int32)).reshape(TOKENS, H * HD)
    group_cols = H * HD // N_MP
    running = residual.astype(jnp.float32)
    for member in range(N_MP):
        head_part = jnp.dot(attended[:, member * group_cols:(member + 1) * group_cols], out_weight[member * group_cols:(member + 1) * group_cols], preferred_element_type=jnp.float32)
        head_part = lax.optimization_barrier(head_part.astype(jnp.bfloat16))
        running = running + head_part.astype(jnp.float32)
    resid_out = running.astype(jnp.bfloat16)
    resid_f32 = resid_out.astype(jnp.float32)
    normed = (resid_f32 * lax.rsqrt(lax.optimization_barrier(jnp.mean(resid_f32 * resid_f32, axis=-1, keepdims=True)) + 1e-06) * norm_gain).astype(jnp.bfloat16)
    lru_in = jnp.dot(normed, lru_weight, preferred_element_type=jnp.float32).astype(jnp.bfloat16)
    seg_int = segment_ids.astype(jnp.int32)
    pad_in = jnp.concatenate([jnp.zeros((CONV - 1, LRU), jnp.bfloat16), lru_in], axis=0)
    pad_conv_seg = jnp.concatenate([jnp.full((CONV - 1,), -1, jnp.int32), seg_int])
    conv_acc = jnp.zeros((TOKENS, LRU), jnp.float32)
    for offset in range(CONV):
        lag_rows = CONV - 1 - offset
        shifted = pad_in[lag_rows:lag_rows + TOKENS].astype(jnp.float32)
        same_doc = (pad_conv_seg[lag_rows:lag_rows + TOKENS] == seg_int)[:, None]
        conv_acc = conv_acc + jnp.where(same_doc, conv_weight[offset] * shifted, 0.0)
    conv_out = conv_acc.astype(jnp.bfloat16)
    grouped = conv_out.reshape(TOKENS, NBLK, BW).astype(jnp.float32)
    decay_gate = jax.nn.sigmoid(jnp.einsum('tbi,bij->tbj', grouped, gate_decay_w.astype(jnp.float32)).reshape(TOKENS, LRU) + gate_decay_b)
    input_gate = jax.nn.sigmoid(jnp.einsum('tbi,bij->tbj', grouped, gate_input_w.astype(jnp.float32)).reshape(TOKENS, LRU) + gate_input_b)
    decay_rate = decay_rates()[decay_codes]
    log_decay = -8.0 * decay_gate * decay_rate
    prev_seg = jnp.concatenate([jnp.full((1,), -1, jnp.int32), seg_int[:-1]])
    restart = (seg_int != prev_seg)[:, None]
    keep_factor = jnp.where(restart, 0.0, jnp.exp(log_decay))
    input_scale = jnp.where(restart, 1.0, jnp.sqrt(-jnp.expm1(2.0 * log_decay)))
    driven = input_scale * input_gate * conv_out.astype(jnp.float32)
    cum_keep, states = lax.associative_scan(chain_link, (keep_factor, driven), axis=0)
    return (resid_out, states.astype(jnp.bfloat16))
```

```python
import math

import jax
import jax.numpy as jnp
from jax import lax
from jax.experimental import pallas as pl
from jax.experimental.pallas import tpu as pltpu
from jax.sharding import PartitionSpec as P

HD = 256
WIN = 2048
CONV = 4
LEVELS = 16
BW = 256


def shifted_2(value, axis, steps):
    count = lax.axis_size(axis)
    initial, last = (max(0, -steps), min(count, count - steps))
    return lax.ppermute(value, axis, [(source, source + steps) for source in range(initial, last)])


def decay_rates():
    levels = jnp.arange(LEVELS, dtype=jnp.float32)
    return 0.006 * jnp.exp(-levels * (math.log(3000.0) / (LEVELS - 1)))


def chain_link(former, latter):
    return (former[0] * latter[0], latter[0] * former[1] + latter[1])


def rms_scaled(values, norm_gain):
    value_f32 = values.astype(jnp.float32)
    inverse = lax.rsqrt(jnp.mean(value_f32 * value_f32, axis=-1, keepdims=True) + 1e-06)
    return (value_f32 * inverse * norm_gain).astype(jnp.bfloat16)


def attend_local(queries, keys_all, allowed):
    rows_here = queries.shape[0]
    heads_here = queries.shape[1] // HD
    query_heads = queries.reshape(rows_here, heads_here, HD)
    score_scale = 1.0 / math.sqrt(HD)
    scores = (
        jnp.einsum("thd,kd->htk", query_heads, keys_all[:, :HD], preferred_element_type=jnp.float32)
        * score_scale
    )
    scores = jnp.where(allowed[None], scores, -1e30)
    row_top = jnp.max(scores, axis=-1, keepdims=True)
    weights = jnp.exp(scores - row_top)
    probs = (weights / jnp.sum(weights, axis=-1, keepdims=True)).astype(jnp.bfloat16)
    gathered = jnp.einsum(
        "htk,kd->thd", probs, keys_all[:, HD:], preferred_element_type=jnp.float32
    )
    return gathered.reshape(rows_here, heads_here * HD).astype(jnp.bfloat16)


def local(
    queries,
    keyvals,
    segment_ids,
    residual,
    out_weight,
    lru_weight,
    conv_weight,
    gate_decay_w,
    gate_input_w,
    gate_decay_b,
    gate_input_b,
    decay_codes,
    norm_gain,
):
    rows_here = queries.shape[0]
    ctx_index = lax.axis_index("ctx")
    back_blocks = WIN // rows_here
    own_kv = lax.all_gather(keyvals, "mp", axis=0, tiled=True)
    earlier = []
    moving = own_kv
    for offset in range(back_blocks):
        moving = shifted_2(moving, "ctx", 1)
        earlier = [moving] + earlier
    keys_all = jnp.concatenate(earlier + [own_kv], axis=0)
    pad_seg = jnp.concatenate([jnp.full((WIN,), -1, jnp.int32), segment_ids])
    query_seg = lax.dynamic_slice_in_dim(segment_ids, ctx_index * rows_here, rows_here)
    key_seg = lax.dynamic_slice_in_dim(
        pad_seg, ctx_index * rows_here, (back_blocks + 1) * rows_here
    )
    query_pos = ctx_index * rows_here + jnp.arange(rows_here, dtype=jnp.int32)
    key_pos = (ctx_index - back_blocks) * rows_here + jnp.arange(
        (back_blocks + 1) * rows_here, dtype=jnp.int32
    )
    distance = query_pos[:, None] - key_pos[None, :]
    allowed = (distance >= 0) & (distance < WIN) & (query_seg[:, None] == key_seg[None, :])
    attended = attend_local(queries, keys_all, allowed)
    head_part = jnp.dot(
        attended,
        lax.all_gather(out_weight, "ctx", axis=1, tiled=True),
        preferred_element_type=jnp.float32,
    )
    summed = lax.psum_scatter(
        head_part.astype(jnp.bfloat16), "mp", scatter_dimension=0, tiled=True
    ).astype(jnp.float32)
    resid_out = (summed + residual.astype(jnp.float32)).astype(jnp.bfloat16)
    normed = lax.all_gather(rms_scaled(resid_out, norm_gain), "mp", axis=0, tiled=True)
    lru_in = jnp.dot(
        normed,
        lax.all_gather(lru_weight, "ctx", axis=0, tiled=True),
        preferred_element_type=jnp.float32,
    ).astype(jnp.bfloat16)
    return resid_out, recurrence(
        lru_in, segment_ids, conv_weight, gate_decay_w, gate_input_w,
        gate_decay_b, gate_input_b, decay_codes,
    )


HALO = 16


def scan_kernel(ext_ref, flags_ref, conv_ref, wd_ref, wi_ref, vec_ref, keep_ref, state_ref):
    rows = state_ref.shape[0]
    groups = rows // 8
    flags = flags_ref[...]
    row_in_group = lax.broadcasted_iota(jnp.int32, (groups, 8, BW), 1)
    for block in range(state_ref.shape[1] // BW):
        cols = slice(block * BW, (block + 1) * BW)
        ext = ext_ref[:, cols].astype(jnp.float32)
        acc = conv_ref[0:1, cols] * ext[HALO:]
        for lag in range(1, CONV):
            moved = pltpu.roll(ext, lag, 0)[HALO:]
            acc = acc + jnp.where(flags[:, lag : lag + 1] > 0.5, conv_ref[lag : lag + 1, cols] * moved, 0.0)
        conv_out = acc.astype(jnp.bfloat16)
        decay_gate = jax.nn.sigmoid(
            jnp.dot(conv_out, wd_ref[block], preferred_element_type=jnp.float32) + vec_ref[0:1, cols]
        )
        input_gate = jax.nn.sigmoid(
            jnp.dot(conv_out, wi_ref[block], preferred_element_type=jnp.float32) + vec_ref[1:2, cols]
        )
        log_decay = -8.0 * decay_gate * vec_ref[2:3, cols]
        restart = flags[:, 0:1] > 0.5
        keep = jnp.where(restart, 0.0, jnp.exp(log_decay))
        x = 2.0 * log_decay
        poly = 1.0 + x * (1.0 / 6.0)
        for order in (5.0, 4.0, 3.0, 2.0):
            poly = 1.0 + x * (1.0 / order) * poly
        scale = jnp.where(restart, 1.0, jnp.sqrt(-x * poly))
        state = scale * input_gate * conv_out.astype(jnp.float32)
        keep = keep.reshape(groups, 8, BW)
        state = state.reshape(groups, 8, BW)
        for shift in (1, 2, 4):
            inside = row_in_group >= shift
            before_state = jnp.where(inside, pltpu.roll(state, shift, 1), 0.0)
            before_keep = jnp.where(inside, pltpu.roll(keep, shift, 1), 1.0)
            state = state + keep * before_state
            keep = keep * before_keep
        keep_carry = jnp.ones((1, BW), jnp.float32)
        state_carry = jnp.zeros((1, BW), jnp.float32)
        for group in range(groups):
            rows_now = slice(group * 8, group * 8 + 8)
            state_now = state[group] + keep[group] * state_carry
            keep_now = keep[group] * keep_carry
            state_ref[rows_now, cols] = state_now
            keep_ref[rows_now, cols] = keep_now
            state_carry = state_now[7:8]
            keep_carry = keep_now[7:8]


def recurrence(
    lru_in, segment_ids, conv_weight, gate_decay_w, gate_input_w, gate_decay_b, gate_input_b, decay_codes
):
    rows_here, channels = lru_in.shape
    ctx_index = lax.axis_index("ctx")
    rim_rows = shifted_2(lru_in[rows_here - HALO :], "ctx", 1)
    extended = jnp.concatenate([rim_rows, lru_in], axis=0)
    pad_seg = jnp.concatenate([jnp.full((CONV - 1,), -1, jnp.int32), segment_ids])
    ext_seg = lax.dynamic_slice_in_dim(pad_seg, ctx_index * rows_here, rows_here + CONV - 1)
    query_seg = ext_seg[CONV - 1 :]
    lagged = [ext_seg[CONV - 1 - lag : CONV - 1 - lag + rows_here] == query_seg for lag in range(CONV)]
    flags = jnp.stack([~lagged[1]] + lagged[1:], axis=1).astype(jnp.float32)
    levels = jnp.arange(LEVELS, dtype=jnp.int32)
    decay_rate = jnp.sum(
        jnp.where(decay_codes[:, None] == levels[None, :], decay_rates()[None, :], 0.0), axis=1
    )
    vectors = jnp.stack([gate_decay_b, gate_input_b, decay_rate])
    full = jax.ShapeDtypeStruct((rows_here, channels), jnp.float32)
    cum_keep, local_state = pl.pallas_call(
        scan_kernel,
        out_shape=(full, full),
        compiler_params=pltpu.CompilerParams(vmem_limit_bytes=40 * 1024 * 1024),
    )(extended, flags, conv_weight, gate_decay_w, gate_input_w, vectors)
    ends = jnp.stack([cum_keep[rows_here - 1], local_state[rows_here - 1]])
    all_ends = lax.all_gather(ends, "ctx", axis=0)
    incoming = jnp.zeros((channels,), jnp.float32)
    for source in range(lax.axis_size("ctx") - 1):
        incoming = jnp.where(
            source < ctx_index, all_ends[source, 0] * incoming + all_ends[source, 1], incoming
        )
    states = local_state + cum_keep * incoming[None, :]
    return states.astype(jnp.bfloat16)


def local_stationary(
    queries,
    keyvals,
    segment_ids,
    residual,
    out_weight,
    lru_weight,
    conv_weight,
    gate_decay_w,
    gate_input_w,
    gate_decay_b,
    gate_input_b,
    decay_codes,
    norm_gain,
):
    rows_here = queries.shape[0]
    tokens = segment_ids.shape[0]
    ctx_index = lax.axis_index("ctx")
    blocks, members = lax.axis_size("ctx"), lax.axis_size("mp")
    piece = rows_here // members
    cols = out_weight.shape[1]
    keys_all = lax.all_gather(keyvals, ("ctx", "mp"), axis=0, tiled=True)
    residual_cols = lax.all_to_all(residual, "ctx", split_axis=1, concat_axis=0, tiled=True)
    query_seg = lax.dynamic_slice_in_dim(segment_ids, ctx_index * rows_here, rows_here)
    query_pos = ctx_index * rows_here + jnp.arange(rows_here, dtype=jnp.int32)
    distance = query_pos[:, None] - jnp.arange(tokens, dtype=jnp.int32)[None, :]
    allowed = (distance >= 0) & (distance < WIN) & (query_seg[:, None] == segment_ids[None, :])
    attended = attend_local(queries, keys_all, allowed)
    attended_all = lax.all_gather(attended, "ctx", axis=0, tiled=True)
    head_part = jnp.dot(attended_all, out_weight, preferred_element_type=jnp.float32)
    summed = lax.psum_scatter(
        head_part.astype(jnp.bfloat16).reshape(blocks, rows_here, cols), "mp", scatter_dimension=1, tiled=True
    )
    resid_cols = (
        summed.reshape(blocks * piece, cols).astype(jnp.float32) + residual_cols.astype(jnp.float32)
    ).astype(jnp.bfloat16)
    resid_out = lax.all_to_all(resid_cols, "ctx", split_axis=0, concat_axis=1, tiled=True)
    resid_f32 = resid_cols.astype(jnp.float32)
    squares = jnp.sum(resid_f32 * resid_f32, axis=-1).reshape(blocks, piece)
    all_squares = lax.all_gather(squares, ("ctx", "mp"), axis=0).reshape(blocks, members, blocks, piece)
    own_squares = lax.dynamic_index_in_dim(all_squares, ctx_index, 2, keepdims=False)
    mean_square = jnp.sum(own_squares, axis=0).reshape(rows_here) / residual.shape[1]
    inverse = lax.rsqrt(mean_square + 1e-06)
    gain = lax.dynamic_slice_in_dim(norm_gain, ctx_index * cols, cols)
    gained = (resid_f32 * gain).astype(jnp.bfloat16).reshape(blocks, piece, cols)
    gained_all = lax.all_gather(gained, "mp", axis=1, tiled=True).reshape(tokens, cols)
    partial = jnp.dot(gained_all, lru_weight, preferred_element_type=jnp.float32).astype(jnp.bfloat16)
    mixed = lax.psum_scatter(partial, "ctx", scatter_dimension=0, tiled=True)
    lru_in = (mixed.astype(jnp.float32) * inverse[:, None]).astype(jnp.bfloat16)
    return resid_out, recurrence(
        lru_in, segment_ids, conv_weight, gate_decay_w, gate_input_w,
        gate_decay_b, gate_input_b, decay_codes,
    )


def solution(mesh):
    in_specs = (
        P(("groups", "ctx"), "mp"),
        P(("groups", "ctx", "mp"), None),
        P("groups"),
        P(("groups", "ctx", "mp"), None),
        P("mp", "ctx"),
        P("ctx", "mp"),
        P(None, "mp"),
        P("mp", None, None),
        P("mp", None, None),
        P("mp"),
        P("mp"),
        P("mp"),
        P(),
    )
    out_specs = (P(("groups", "ctx", "mp"), None), P(("groups", "ctx"), "mp"))

    def body(*args):
        segment_ids, out_weight = args[2], args[4]
        stationary = segment_ids.shape[0] <= lax.axis_size("ctx") * out_weight.shape[1] // 2
        return (local_stationary if stationary else local)(*args)

    return jax.shard_map(body, mesh=mesh, in_specs=in_specs, out_specs=out_specs, check_vma=False)
```

```python
import functools
import math

import jax
import jax.numpy as jnp
from jax import lax
from jax.experimental import pallas as pl
from jax.experimental.pallas import tpu as pltpu
from jax.sharding import PartitionSpec as P

HD = 256
WIN = 2048
CONV = 4
LEVELS = 16
BW = 256


def shifted_2(value, axis, steps):
    count = lax.axis_size(axis)
    initial, last = (max(0, -steps), min(count, count - steps))
    return lax.ppermute(value, axis, [(source, source + steps) for source in range(initial, last)])


def decay_rates():
    levels = jnp.arange(LEVELS, dtype=jnp.float32)
    return 0.006 * jnp.exp(-levels * (math.log(3000.0) / (LEVELS - 1)))


def chain_link(former, latter):
    return (former[0] * latter[0], latter[0] * former[1] + latter[1])


def rms_scaled(values, norm_gain):
    value_f32 = values.astype(jnp.float32)
    inverse = lax.rsqrt(jnp.mean(value_f32 * value_f32, axis=-1, keepdims=True) + 1e-06)
    return (value_f32 * inverse * norm_gain).astype(jnp.bfloat16)


def attend_local(queries, keys_all, allowed):
    rows_here = queries.shape[0]
    heads_here = queries.shape[1] // HD
    query_heads = queries.reshape(rows_here, heads_here, HD)
    score_scale = 1.0 / math.sqrt(HD)
    scores = (
        jnp.einsum("thd,kd->htk", query_heads, keys_all[:, :HD], preferred_element_type=jnp.float32)
        * score_scale
    )
    scores = jnp.where(allowed[None], scores, -1e30)
    row_top = jnp.max(scores, axis=-1, keepdims=True)
    weights = jnp.exp(scores - row_top)
    probs = (weights / jnp.sum(weights, axis=-1, keepdims=True)).astype(jnp.bfloat16)
    gathered = jnp.einsum(
        "htk,kd->thd", probs, keys_all[:, HD:], preferred_element_type=jnp.float32
    )
    return gathered.reshape(rows_here, heads_here * HD).astype(jnp.bfloat16)


def local(
    queries,
    keyvals,
    segment_ids,
    residual,
    out_weight,
    lru_weight,
    conv_weight,
    gate_decay_w,
    gate_input_w,
    gate_decay_b,
    gate_input_b,
    decay_codes,
    norm_gain,
):
    rows_here = queries.shape[0]
    ctx_index = lax.axis_index("ctx")
    back_blocks = WIN // rows_here
    own_kv = lax.all_gather(keyvals, "mp", axis=0, tiled=True)
    earlier = []
    moving = own_kv
    for offset in range(back_blocks):
        moving = shifted_2(moving, "ctx", 1)
        earlier = [moving] + earlier
    keys_all = jnp.concatenate(earlier + [own_kv], axis=0)
    pad_seg = jnp.concatenate([jnp.full((WIN,), -1, jnp.int32), segment_ids])
    query_seg = lax.dynamic_slice_in_dim(segment_ids, ctx_index * rows_here, rows_here)
    key_seg = lax.dynamic_slice_in_dim(
        pad_seg, ctx_index * rows_here, (back_blocks + 1) * rows_here
    )
    query_pos = ctx_index * rows_here + jnp.arange(rows_here, dtype=jnp.int32)
    key_pos = (ctx_index - back_blocks) * rows_here + jnp.arange(
        (back_blocks + 1) * rows_here, dtype=jnp.int32
    )
    distance = query_pos[:, None] - key_pos[None, :]
    allowed = (distance >= 0) & (distance < WIN) & (query_seg[:, None] == key_seg[None, :])
    attended = attend_local(queries, keys_all, allowed)
    head_part = jnp.dot(
        attended,
        lax.all_gather(out_weight, "ctx", axis=1, tiled=True),
        preferred_element_type=jnp.float32,
    )
    summed = lax.psum_scatter(
        head_part.astype(jnp.bfloat16), "mp", scatter_dimension=0, tiled=True
    ).astype(jnp.float32)
    resid_out = (summed + residual.astype(jnp.float32)).astype(jnp.bfloat16)
    normed = lax.all_gather(rms_scaled(resid_out, norm_gain), "mp", axis=0, tiled=True)
    lru_in = jnp.dot(
        normed,
        lax.all_gather(lru_weight, "ctx", axis=0, tiled=True),
        preferred_element_type=jnp.float32,
    ).astype(jnp.bfloat16)
    return resid_out, recurrence(
        lru_in, segment_ids, conv_weight, gate_decay_w, gate_input_w,
        gate_decay_b, gate_input_b, decay_codes,
    )


HALO = 16


def scan_kernel(ext_ref, flags_ref, conv_ref, wd_ref, wi_ref, vec_ref, keep_ref, state_ref):
    rows = state_ref.shape[0]
    groups = rows // 8
    flags = flags_ref[...]
    row_in_group = lax.broadcasted_iota(jnp.int32, (groups, 8, BW), 1)
    for block in range(state_ref.shape[1] // BW):
        cols = slice(block * BW, (block + 1) * BW)
        ext = ext_ref[:, cols].astype(jnp.float32)
        acc = conv_ref[0:1, cols] * ext[HALO:]
        for lag in range(1, CONV):
            moved = pltpu.roll(ext, lag, 0)[HALO:]
            acc = acc + jnp.where(flags[:, lag : lag + 1] > 0.5, conv_ref[lag : lag + 1, cols] * moved, 0.0)
        conv_out = acc.astype(jnp.bfloat16)
        decay_gate = jax.nn.sigmoid(
            jnp.dot(conv_out, wd_ref[block], preferred_element_type=jnp.float32) + vec_ref[0:1, cols]
        )
        input_gate = jax.nn.sigmoid(
            jnp.dot(conv_out, wi_ref[block], preferred_element_type=jnp.float32) + vec_ref[1:2, cols]
        )
        log_decay = -8.0 * decay_gate * vec_ref[2:3, cols]
        restart = flags[:, 0:1] > 0.5
        keep = jnp.where(restart, 0.0, jnp.exp(log_decay))
        x = 2.0 * log_decay
        poly = 1.0 + x * (1.0 / 6.0)
        for order in (5.0, 4.0, 3.0, 2.0):
            poly = 1.0 + x * (1.0 / order) * poly
        scale = jnp.where(restart, 1.0, jnp.sqrt(-x * poly))
        state = scale * input_gate * conv_out.astype(jnp.float32)
        keep = keep.reshape(groups, 8, BW)
        state = state.reshape(groups, 8, BW)
        for shift in (1, 2, 4):
            inside = row_in_group >= shift
            before_state = jnp.where(inside, pltpu.roll(state, shift, 1), 0.0)
            before_keep = jnp.where(inside, pltpu.roll(keep, shift, 1), 1.0)
            state = state + keep * before_state
            keep = keep * before_keep
        keep_carry = jnp.ones((1, BW), jnp.float32)
        state_carry = jnp.zeros((1, BW), jnp.float32)
        for group in range(groups):
            rows_now = slice(group * 8, group * 8 + 8)
            state_now = state[group] + keep[group] * state_carry
            keep_now = keep[group] * keep_carry
            state_ref[rows_now, cols] = state_now
            keep_ref[rows_now, cols] = keep_now
            state_carry = state_now[7:8]
            keep_carry = keep_now[7:8]


def recurrence_inputs(rows_here, segment_ids, gate_decay_b, gate_input_b, decay_codes):
    ctx_index = lax.axis_index("ctx")
    pad_seg = jnp.concatenate([jnp.full((CONV - 1,), -1, jnp.int32), segment_ids])
    ext_seg = lax.dynamic_slice_in_dim(pad_seg, ctx_index * rows_here, rows_here + CONV - 1)
    query_seg = ext_seg[CONV - 1 :]
    lagged = [ext_seg[CONV - 1 - lag : CONV - 1 - lag + rows_here] == query_seg for lag in range(CONV)]
    flags = jnp.stack([~lagged[1]] + lagged[1:], axis=1).astype(jnp.float32)
    levels = jnp.arange(LEVELS, dtype=jnp.int32)
    decay_rate = jnp.sum(
        jnp.where(decay_codes[:, None] == levels[None, :], decay_rates()[None, :], 0.0), axis=1
    )
    vectors = jnp.stack([gate_decay_b, gate_input_b, decay_rate])
    return flags, vectors, query_seg


def recurrence(
    lru_in, segment_ids, conv_weight, gate_decay_w, gate_input_w, gate_decay_b, gate_input_b, decay_codes
):
    rows_here, channels = lru_in.shape
    ctx_index = lax.axis_index("ctx")
    rim_rows = shifted_2(lru_in[rows_here - HALO :], "ctx", 1)
    extended = jnp.concatenate([rim_rows, lru_in], axis=0)
    flags, vectors, _ = recurrence_inputs(rows_here, segment_ids, gate_decay_b, gate_input_b, decay_codes)
    full = jax.ShapeDtypeStruct((rows_here, channels), jnp.float32)
    cum_keep, local_state = pl.pallas_call(
        scan_kernel,
        out_shape=(full, full),
        compiler_params=pltpu.CompilerParams(vmem_limit_bytes=40 * 1024 * 1024),
    )(extended, flags, conv_weight, gate_decay_w, gate_input_w, vectors)
    ends = jnp.stack([cum_keep[rows_here - 1], local_state[rows_here - 1]])
    all_ends = lax.all_gather(ends, "ctx", axis=0)
    incoming = jnp.zeros((channels,), jnp.float32)
    for source in range(lax.axis_size("ctx") - 1):
        incoming = jnp.where(
            source < ctx_index, all_ends[source, 0] * incoming + all_ends[source, 1], incoming
        )
    states = local_state + cum_keep * incoming[None, :]
    return states.astype(jnp.bfloat16)


def fused_kernel(
    blocks, members, q_ref, kv_ref, qseg_ref, kseg_ref, res_ref, ow_ref, lw_ref, gain_ref, flags_ref,
    conv_ref, wd_ref, wi_ref, vec_ref, resid_ref, lru_ref,
    kv_all, att, heads, sums, gained, partial, mixed, resid_in, resid_rows, inverse, ext, rim, ends, keep, state,
    kv_z, kv_x, att_s, res_s, sum_s, gain_s, row_s, mix_s, inv_s, rim_s, end_s,
):
    group, c, m = lax.axis_index("groups"), lax.axis_index("ctx"), lax.axis_index("mp")
    rows, cols = q_ref.shape
    piece = rows // members
    width = ow_ref.shape[1]

    def ahead(offset):
        return lax.rem(c + offset, blocks)

    def behind(offset):
        return lax.rem(c + blocks - offset, blocks)

    def member(offset):
        return lax.rem(m + offset, members)

    def rows_of(which):
        return pl.ds(pl.multiple_of(which * piece, piece), piece)

    def cols_of(which):
        return pl.ds(pl.multiple_of(which * width, width), width)

    def send(src, dst, sems, index, to_c, to_m):
        return pltpu.make_async_remote_copy(
            src_ref=src, dst_ref=dst, send_sem=sems.at[(0, *index)], recv_sem=sems.at[(1, *index)],
            device_id=(group, to_c, to_m), device_id_type=pl.DeviceIdType.MESH,
        )

    def kv_z_copy(i):
        slot = kv_all.at[c * members + m]
        return send(kv_ref, slot, kv_z, (i,), ahead(i), m)

    def kv_x_copy(i, j):
        slot = kv_all.at[behind(i) * members + m]
        return send(slot, slot, kv_x, (i, j), c, member(j))

    def res_copy(i):
        return send(res_ref.at[:, cols_of(behind(i))], resid_in.at[i], res_s, (i,), behind(i), m)

    def att_copy(i):
        return send(att.at[0], att.at[i], att_s, (i,), behind(i), m)

    def sum_copy(i, j):
        return send(heads.at[i, rows_of(member(j))], sums.at[i, m], sum_s, (i, j), c, member(j))

    def gain_copy(i, j):
        return send(gained.at[i, rows_of(m)], gained.at[i, rows_of(m)], gain_s, (i, j), c, member(j))

    def row_copy(i):
        return send(resid_in.at[i], resid_rows.at[c], row_s, (i,), ahead(i), m)

    def mix_copy(i):
        return send(partial.at[i], mixed.at[i], mix_s, (i,), ahead(i), m)

    def inv_copy(j):
        return send(inverse.at[m], inverse.at[m], inv_s, (j,), c, member(j))

    def rim_copy():
        return send(ext.at[pl.ds(rows, HALO)], rim, rim_s, (0,), ahead(1), m)

    def end_copy(i):
        return send(ends.at[c], ends.at[c], end_s, (i,), ahead(i), m)

    barrier = pltpu.get_barrier_semaphore()
    for i in range(blocks):
        for j in range(members):
            if i or j:
                pl.semaphore_signal(
                    barrier, inc=1, device_id=(group, ahead(i), member(j)), device_id_type=pl.DeviceIdType.MESH
                )
    pl.semaphore_wait(barrier, blocks * members - 1)

    kv_all[c * members + m] = kv_ref[...]
    for i in range(1, blocks):
        kv_z_copy(i).start()
    for j in range(1, members):
        kv_x_copy(0, j).start()
    for i in range(1, blocks):
        res_copy(i).start()
    resid_in[0] = res_ref[:, cols_of(c)]
    for i in range(1, blocks):
        kv_z_copy(i).wait_recv()
        for j in range(1, members):
            kv_x_copy(i, j).start()
    for i in range(blocks):
        for j in range(1, members):
            kv_x_copy(i, j).wait_recv()

    tokens = kseg_ref.shape[1]
    distance = (
        c * rows
        + lax.broadcasted_iota(jnp.int32, (rows, tokens), 0)
        - lax.broadcasted_iota(jnp.int32, (rows, tokens), 1)
    )
    allowed = (distance >= 0) & (distance < WIN) & (qseg_ref[...] == kseg_ref[...])
    keys_all = kv_all[...].reshape(tokens, 2 * HD)
    for head in range(cols // HD):
        span = slice(head * HD, (head + 1) * HD)
        scores = lax.dot_general(
            q_ref[:, span], keys_all[:, :HD], (((1,), (1,)), ((), ())), preferred_element_type=jnp.float32
        ) * (1.0 / math.sqrt(HD))
        scores = jnp.where(allowed, scores, -1e30)
        weights = jnp.exp(scores - jnp.max(scores, axis=-1, keepdims=True))
        probs = (weights / jnp.sum(weights, axis=-1, keepdims=True)).astype(jnp.bfloat16)
        att[0, :, span] = jnp.dot(probs, keys_all[:, HD:], preferred_element_type=jnp.float32).astype(jnp.bfloat16)
    for i in range(1, blocks):
        att_copy(i).start()

    tile = math.gcd(width, 256)

    def multiply(source, weight, target, i):
        @pl.loop(0, weight.shape[1] // tile)
        def _(n):
            span = pl.ds(pl.multiple_of(n * tile, tile), tile)
            target[i, :, span] = jnp.dot(
                source[i], weight[:, span], preferred_element_type=jnp.float32
            ).astype(jnp.bfloat16)

    @pl.loop(0, blocks + 2)
    def _(tick):
        @pl.when(tick < blocks)
        def _():
            @pl.when(tick > 0)
            def _():
                att_copy(tick).wait_recv()

            multiply(att, ow_ref, heads, tick)
            for j in range(1, members):
                sum_copy(tick, j).start()

        @pl.when((tick > 0) & (tick < blocks + 1))
        def _():
            i = tick - 1
            sums[i, m] = heads[i, rows_of(m)]

            @pl.when(i > 0)
            def _():
                res_copy(i).wait_recv()

            total = resid_in[i].astype(jnp.float32)
            for j in range(1, members):
                sum_copy(i, j).wait_recv()
            for j in range(members):
                total = total + sums[i, j].astype(jnp.float32)
            resid = total.astype(jnp.bfloat16)
            gained[i, rows_of(m)] = (resid.astype(jnp.float32) * gain_ref[...]).astype(jnp.bfloat16)
            for j in range(1, members):
                gain_copy(i, j).start()
            resid_in[i] = resid

            @pl.when(i > 0)
            def _():
                row_copy(i).start()

        @pl.when(tick > 1)
        def _():
            i = tick - 2
            for j in range(1, members):
                gain_copy(i, j).wait_recv()
            multiply(gained, lw_ref, partial, i)

            @pl.when(i > 0)
            def _():
                mix_copy(i).start()

    resid_rows[c] = resid_in[0]
    for i in range(1, blocks):
        row_copy(i).wait_recv()
    squares = jnp.zeros((piece, 1), jnp.float32)
    for k in range(blocks):
        resid = resid_rows[k]
        resid_ref[:, k * width : (k + 1) * width] = resid
        resid_f32 = resid.astype(jnp.float32)
        squares = squares + jnp.sum(resid_f32 * resid_f32, axis=-1, keepdims=True)
    inverse[m] = jnp.broadcast_to(lax.rsqrt(squares / (blocks * width) + 1e-06), inverse.shape[1:])
    for j in range(1, members):
        inv_copy(j).start()
    for i in range(1, blocks):
        mix_copy(i).wait_recv()
    for j in range(1, members):
        inv_copy(j).wait_recv()
    scale = inverse[...].reshape(rows, inverse.shape[2])[:, 0:1]
    total = partial[0].astype(jnp.float32)
    for i in range(1, blocks):
        total = total + mixed[i].astype(jnp.float32)
    ext[HALO:] = (total * scale).astype(jnp.bfloat16)
    rim_copy().start()
    rim_copy().wait()
    ext[:HALO] = rim[...]

    scan_kernel(ext, flags_ref, conv_ref, wd_ref, wi_ref, vec_ref, keep, state)

    ends[c, 0:8] = keep[rows - 8 :]
    ends[c, 8:16] = state[rows - 8 :]
    for i in range(1, blocks):
        end_copy(i).start()
    for i in range(1, blocks):
        end_copy(i).wait_recv()
    incoming = jnp.zeros((1, keep.shape[1]), jnp.float32)
    for source in range(blocks - 1):
        incoming = jnp.where(source < c, ends[source, 7:8] * incoming + ends[source, 15:16], incoming)
    lru_ref[...] = (state[...] + keep[...] * incoming).astype(jnp.bfloat16)

    for j in range(1, members):
        inv_copy(j).wait_send()
    for i in range(blocks):
        for j in range(1, members):
            kv_x_copy(i, j).wait_send()
            sum_copy(i, j).wait_send()
            gain_copy(i, j).wait_send()
        if i:
            kv_z_copy(i).wait_send()
            res_copy(i).wait_send()
            att_copy(i).wait_send()
            row_copy(i).wait_send()
            mix_copy(i).wait_send()
            end_copy(i).wait_send()


def local_stationary(
    queries,
    keyvals,
    segment_ids,
    residual,
    out_weight,
    lru_weight,
    conv_weight,
    gate_decay_w,
    gate_input_w,
    gate_decay_b,
    gate_input_b,
    decay_codes,
    norm_gain,
):
    rows, cols = queries.shape
    blocks, members = lax.axis_size("ctx"), lax.axis_size("mp")
    piece = rows // members
    width, channels = out_weight.shape[1], lru_weight.shape[1]
    ctx_index = lax.axis_index("ctx")
    flags, vectors, query_seg = recurrence_inputs(rows, segment_ids, gate_decay_b, gate_input_b, decay_codes)
    gain = lax.dynamic_slice_in_dim(norm_gain, ctx_index * width, width)[None]
    bf16, f32 = jnp.bfloat16, jnp.float32
    vmem = pl.BlockSpec(memory_space=pltpu.VMEM)
    sems = [(blocks,), (blocks, members), (blocks,), (blocks,), (blocks, members), (blocks, members)]
    sems = sems + [(blocks,), (blocks,), (members,), (1,), (blocks,)]
    return pl.pallas_call(
        functools.partial(fused_kernel, blocks, members),
        out_shape=(jax.ShapeDtypeStruct(residual.shape, bf16), jax.ShapeDtypeStruct((rows, channels), bf16)),
        in_specs=[vmem] * 13,
        out_specs=(vmem, vmem),
        scratch_shapes=[
            pltpu.VMEM((blocks * members,) + keyvals.shape, bf16),
            pltpu.VMEM((blocks, rows, cols), bf16),
            pltpu.VMEM((blocks, rows, width), bf16),
            pltpu.VMEM((blocks, members, piece, width), bf16),
            pltpu.VMEM((blocks, rows, width), bf16),
            pltpu.VMEM((blocks, rows, channels), bf16),
            pltpu.VMEM((blocks, rows, channels), bf16),
            pltpu.VMEM((blocks, piece, width), bf16),
            pltpu.VMEM((blocks, piece, width), bf16),
            pltpu.VMEM((members, piece, 128), f32),
            pltpu.VMEM((rows + HALO, channels), bf16),
            pltpu.VMEM((HALO, channels), bf16),
            pltpu.VMEM((blocks, 16, channels), f32),
            pltpu.VMEM((rows, channels), f32),
            pltpu.VMEM((rows, channels), f32),
        ]
        + [pltpu.SemaphoreType.DMA((2,) + shape) for shape in sems],
        compiler_params=pltpu.CompilerParams(
            collective_id=0, has_side_effects=True, vmem_limit_bytes=56 * 1024 * 1024
        ),
    )(
        queries, keyvals, query_seg[:, None], segment_ids[None], residual, out_weight, lru_weight, gain,
        flags, conv_weight, gate_decay_w, gate_input_w, vectors,
    )


def solution(mesh):
    in_specs = (
        P(("groups", "ctx"), "mp"),
        P(("groups", "ctx", "mp"), None),
        P("groups"),
        P(("groups", "ctx", "mp"), None),
        P("mp", "ctx"),
        P("ctx", "mp"),
        P(None, "mp"),
        P("mp", None, None),
        P("mp", None, None),
        P("mp"),
        P("mp"),
        P("mp"),
        P(),
    )
    out_specs = (P(("groups", "ctx", "mp"), None), P(("groups", "ctx"), "mp"))

    def body(*args):
        segment_ids, out_weight = args[2], args[4]
        stationary = segment_ids.shape[0] <= lax.axis_size("ctx") * out_weight.shape[1] // 2
        return (local_stationary if stationary else local)(*args)

    return jax.shard_map(body, mesh=mesh, in_specs=in_specs, out_specs=out_specs, check_vma=False)
```

```python
import functools
import math

import jax
import jax.numpy as jnp
from jax import lax
from jax.experimental import pallas as pl
from jax.experimental.pallas import tpu as pltpu
from jax.sharding import PartitionSpec as P

HD = 256
WIN = 2048
CONV = 4
LEVELS = 16
BW = 256


def shifted_2(value, axis, steps):
    count = lax.axis_size(axis)
    initial, last = (max(0, -steps), min(count, count - steps))
    return lax.ppermute(value, axis, [(source, source + steps) for source in range(initial, last)])


def decay_rates():
    levels = jnp.arange(LEVELS, dtype=jnp.float32)
    return 0.006 * jnp.exp(-levels * (math.log(3000.0) / (LEVELS - 1)))


def chain_link(former, latter):
    return (former[0] * latter[0], latter[0] * former[1] + latter[1])


def rms_scaled(values, norm_gain):
    value_f32 = values.astype(jnp.float32)
    inverse = lax.rsqrt(jnp.mean(value_f32 * value_f32, axis=-1, keepdims=True) + 1e-06)
    return (value_f32 * inverse * norm_gain).astype(jnp.bfloat16)


def attend_local(queries, keys_all, allowed):
    rows_here = queries.shape[0]
    heads_here = queries.shape[1] // HD
    query_heads = queries.reshape(rows_here, heads_here, HD)
    score_scale = 1.0 / math.sqrt(HD)
    scores = (
        jnp.einsum("thd,kd->htk", query_heads, keys_all[:, :HD], preferred_element_type=jnp.float32)
        * score_scale
    )
    scores = jnp.where(allowed[None], scores, -1e30)
    row_top = jnp.max(scores, axis=-1, keepdims=True)
    weights = jnp.exp(scores - row_top)
    probs = (weights / jnp.sum(weights, axis=-1, keepdims=True)).astype(jnp.bfloat16)
    gathered = jnp.einsum(
        "htk,kd->thd", probs, keys_all[:, HD:], preferred_element_type=jnp.float32
    )
    return gathered.reshape(rows_here, heads_here * HD).astype(jnp.bfloat16)


def local(
    queries,
    keyvals,
    segment_ids,
    residual,
    out_weight,
    lru_weight,
    conv_weight,
    gate_decay_w,
    gate_input_w,
    gate_decay_b,
    gate_input_b,
    decay_codes,
    norm_gain,
):
    rows_here = queries.shape[0]
    ctx_index = lax.axis_index("ctx")
    back_blocks = WIN // rows_here
    own_kv = lax.all_gather(keyvals, "mp", axis=0, tiled=True)
    earlier = []
    moving = own_kv
    for offset in range(back_blocks):
        moving = shifted_2(moving, "ctx", 1)
        earlier = [moving] + earlier
    keys_all = jnp.concatenate(earlier + [own_kv], axis=0)
    pad_seg = jnp.concatenate([jnp.full((WIN,), -1, jnp.int32), segment_ids])
    query_seg = lax.dynamic_slice_in_dim(segment_ids, ctx_index * rows_here, rows_here)
    key_seg = lax.dynamic_slice_in_dim(
        pad_seg, ctx_index * rows_here, (back_blocks + 1) * rows_here
    )
    query_pos = ctx_index * rows_here + jnp.arange(rows_here, dtype=jnp.int32)
    key_pos = (ctx_index - back_blocks) * rows_here + jnp.arange(
        (back_blocks + 1) * rows_here, dtype=jnp.int32
    )
    distance = query_pos[:, None] - key_pos[None, :]
    allowed = (distance >= 0) & (distance < WIN) & (query_seg[:, None] == key_seg[None, :])
    attended = attend_local(queries, keys_all, allowed)
    head_part = jnp.dot(
        attended,
        lax.all_gather(out_weight, "ctx", axis=1, tiled=True),
        preferred_element_type=jnp.float32,
    )
    summed = lax.psum_scatter(
        head_part.astype(jnp.bfloat16), "mp", scatter_dimension=0, tiled=True
    ).astype(jnp.float32)
    resid_out = (summed + residual.astype(jnp.float32)).astype(jnp.bfloat16)
    normed = lax.all_gather(rms_scaled(resid_out, norm_gain), "mp", axis=0, tiled=True)
    lru_in = jnp.dot(
        normed,
        lax.all_gather(lru_weight, "ctx", axis=0, tiled=True),
        preferred_element_type=jnp.float32,
    ).astype(jnp.bfloat16)
    return resid_out, recurrence(
        lru_in, segment_ids, conv_weight, gate_decay_w, gate_input_w,
        gate_decay_b, gate_input_b, decay_codes,
    )


HALO = 16


def scan_kernel(ext_ref, flags_ref, conv_ref, wd_ref, wi_ref, vec_ref, keep_ref, state_ref):
    rows = state_ref.shape[0]
    groups = rows // 8
    flags = flags_ref[...]
    row_in_group = lax.broadcasted_iota(jnp.int32, (groups, 8, BW), 1)
    for block in range(state_ref.shape[1] // BW):
        cols = slice(block * BW, (block + 1) * BW)
        ext = ext_ref[:, cols].astype(jnp.float32)
        acc = conv_ref[0:1, cols] * ext[HALO:]
        for lag in range(1, CONV):
            moved = pltpu.roll(ext, lag, 0)[HALO:]
            acc = acc + jnp.where(flags[:, lag : lag + 1] > 0.5, conv_ref[lag : lag + 1, cols] * moved, 0.0)
        conv_out = acc.astype(jnp.bfloat16)
        decay_gate = jax.nn.sigmoid(
            jnp.dot(conv_out, wd_ref[block], preferred_element_type=jnp.float32) + vec_ref[0:1, cols]
        )
        input_gate = jax.nn.sigmoid(
            jnp.dot(conv_out, wi_ref[block], preferred_element_type=jnp.float32) + vec_ref[1:2, cols]
        )
        log_decay = -8.0 * decay_gate * vec_ref[2:3, cols]
        restart = flags[:, 0:1] > 0.5
        keep = jnp.where(restart, 0.0, jnp.exp(log_decay))
        x = 2.0 * log_decay
        poly = 1.0 + x * (1.0 / 6.0)
        for order in (5.0, 4.0, 3.0, 2.0):
            poly = 1.0 + x * (1.0 / order) * poly
        scale = jnp.where(restart, 1.0, jnp.sqrt(-x * poly))
        state = scale * input_gate * conv_out.astype(jnp.float32)
        keep = keep.reshape(groups, 8, BW)
        state = state.reshape(groups, 8, BW)
        for shift in (1, 2, 4):
            inside = row_in_group >= shift
            before_state = jnp.where(inside, pltpu.roll(state, shift, 1), 0.0)
            before_keep = jnp.where(inside, pltpu.roll(keep, shift, 1), 1.0)
            state = state + keep * before_state
            keep = keep * before_keep
        keep_carry = jnp.ones((1, BW), jnp.float32)
        state_carry = jnp.zeros((1, BW), jnp.float32)
        for group in range(groups):
            rows_now = slice(group * 8, group * 8 + 8)
            state_now = state[group] + keep[group] * state_carry
            keep_now = keep[group] * keep_carry
            state_ref[rows_now, cols] = state_now
            keep_ref[rows_now, cols] = keep_now
            state_carry = state_now[7:8]
            keep_carry = keep_now[7:8]


def recurrence_inputs(rows_here, segment_ids, gate_decay_b, gate_input_b, decay_codes):
    ctx_index = lax.axis_index("ctx")
    pad_seg = jnp.concatenate([jnp.full((CONV - 1,), -1, jnp.int32), segment_ids])
    ext_seg = lax.dynamic_slice_in_dim(pad_seg, ctx_index * rows_here, rows_here + CONV - 1)
    query_seg = ext_seg[CONV - 1 :]
    lagged = [ext_seg[CONV - 1 - lag : CONV - 1 - lag + rows_here] == query_seg for lag in range(CONV)]
    flags = jnp.stack([~lagged[1]] + lagged[1:], axis=1).astype(jnp.float32)
    levels = jnp.arange(LEVELS, dtype=jnp.int32)
    decay_rate = jnp.sum(
        jnp.where(decay_codes[:, None] == levels[None, :], decay_rates()[None, :], 0.0), axis=1
    )
    vectors = jnp.stack([gate_decay_b, gate_input_b, decay_rate])
    return flags, vectors, query_seg


def recurrence(
    lru_in, segment_ids, conv_weight, gate_decay_w, gate_input_w, gate_decay_b, gate_input_b, decay_codes
):
    rows_here, channels = lru_in.shape
    ctx_index = lax.axis_index("ctx")
    rim_rows = shifted_2(lru_in[rows_here - HALO :], "ctx", 1)
    extended = jnp.concatenate([rim_rows, lru_in], axis=0)
    flags, vectors, _ = recurrence_inputs(rows_here, segment_ids, gate_decay_b, gate_input_b, decay_codes)
    full = jax.ShapeDtypeStruct((rows_here, channels), jnp.float32)
    cum_keep, local_state = pl.pallas_call(
        scan_kernel,
        out_shape=(full, full),
        compiler_params=pltpu.CompilerParams(vmem_limit_bytes=40 * 1024 * 1024),
    )(extended, flags, conv_weight, gate_decay_w, gate_input_w, vectors)
    ends = jnp.stack([cum_keep[rows_here - 1], local_state[rows_here - 1]])
    all_ends = lax.all_gather(ends, "ctx", axis=0)
    incoming = jnp.zeros((channels,), jnp.float32)
    for source in range(lax.axis_size("ctx") - 1):
        incoming = jnp.where(
            source < ctx_index, all_ends[source, 0] * incoming + all_ends[source, 1], incoming
        )
    states = local_state + cum_keep * incoming[None, :]
    return states.astype(jnp.bfloat16)


def fused_kernel(
    blocks, members, q_ref, kv_ref, qseg_ref, kseg_ref, res_ref, ow_ref, lw_ref, gain_ref, flags_ref,
    conv_ref, wd_ref, wi_ref, vec_ref, resid_ref, lru_ref,
    kv_all, att, heads, sums, gained, partial, mixed, resid_in, resid_rows, inverse, ext, rim, ends, keep, state,
    kv_z, kv_x, att_s, res_s, sum_s, gain_s, row_s, mix_s, inv_s, rim_s, end_s,
):
    group, c, m = lax.axis_index("groups"), lax.axis_index("ctx"), lax.axis_index("mp")
    rows, cols = q_ref.shape
    piece = rows // members
    width = ow_ref.shape[1]

    def ahead(offset):
        return lax.rem(c + offset, blocks)

    def behind(offset):
        return lax.rem(c + blocks - offset, blocks)

    def member(offset):
        return lax.rem(m + offset, members)

    def rows_of(which):
        return pl.ds(pl.multiple_of(which * piece, piece), piece)

    def cols_of(which):
        return pl.ds(pl.multiple_of(which * width, width), width)

    def send(src, dst, sems, index, to_c, to_m, landing=None):
        landing = index if landing is None else landing
        return pltpu.make_async_remote_copy(
            src_ref=src, dst_ref=dst, send_sem=sems.at[(0, *index)], recv_sem=sems.at[(1, *landing)],
            device_id=(group, to_c, to_m), device_id_type=pl.DeviceIdType.MESH,
        )

    def kv_z_copy(i):
        slot = kv_all.at[c * members + m]
        return send(kv_ref, slot, kv_z, (i,), ahead(i), m)

    def kv_x_copy(i, j):
        slot = kv_all.at[behind(i) * members + m]
        return send(slot, slot, kv_x, (i, j), c, member(j))

    def res_copy(i):
        return send(res_ref.at[:, cols_of(ahead(i))], resid_in.at[c], res_s, (i,), ahead(i), m, (c,))

    def res_arrival(b):
        return send(res_ref.at[:, cols_of(c)], resid_in.at[b], res_s, (0,), b, m, (b,))

    def att_right(b):
        return send(att.at[b], att.at[b], att_s, (b,), ahead(1), m)

    def att_left(b):
        return send(att.at[b], att.at[b], att_s, (b + blocks,), behind(1), m, (b,))

    def relay(b, act):
        @pl.when((b <= c) & (c < blocks - 1))
        def _():
            act(att_right(b))

        @pl.when((b >= c) & (c > 0))
        def _():
            act(att_left(b))

    nearer = jnp.minimum(c, blocks - 1 - c)

    def block_at(tick):
        both = tick <= 2 * nearer
        steps = jnp.where(both, lax.div(tick + 1, 2), tick - nearer)
        leftward = jnp.where(both, lax.rem(tick, 2) == 1, c > nearer)
        return jnp.where(leftward, c - steps, c + steps)

    def sum_copy(i, j):
        return send(heads.at[i, rows_of(member(j))], sums.at[i, m], sum_s, (i, j), c, member(j))

    def gain_copy(i, j):
        return send(gained.at[i, rows_of(m)], gained.at[i, rows_of(m)], gain_s, (i, j), c, member(j))

    def row_copy(b):
        return send(resid_in.at[b], resid_rows.at[c], row_s, (b,), b, m, (c,))

    def mix_copy(i, b):
        return send(partial.at[i], mixed.at[c], mix_s, (b,), b, m, (c,))

    def row_arrival(i):
        return send(resid_in.at[0], resid_rows.at[c], row_s, (0,), ahead(i), m, (ahead(i),))

    def mix_arrival(i):
        return send(partial.at[0], mixed.at[c], mix_s, (0,), ahead(i), m, (ahead(i),))

    def inv_copy(j):
        return send(inverse.at[m], inverse.at[m], inv_s, (j,), c, member(j))

    def rim_copy():
        return send(ext.at[pl.ds(rows, HALO)], rim, rim_s, (0,), ahead(1), m)

    def end_copy(i):
        return send(ends.at[c], ends.at[c], end_s, (i,), ahead(i), m)

    barrier = pltpu.get_barrier_semaphore()
    for i in range(blocks):
        for j in range(members):
            if i or j:
                pl.semaphore_signal(
                    barrier, inc=1, device_id=(group, ahead(i), member(j)), device_id_type=pl.DeviceIdType.MESH
                )
    pl.semaphore_wait(barrier, blocks * members - 1)

    kv_all[c * members + m] = kv_ref[...]
    for i in range(1, blocks):
        kv_z_copy(i).start()
    for j in range(1, members):
        kv_x_copy(0, j).start()
    for i in range(1, blocks):
        res_copy(i).start()
    resid_in[c] = res_ref[:, cols_of(c)]
    for i in range(1, blocks):
        kv_z_copy(i).wait_recv()
        for j in range(1, members):
            kv_x_copy(i, j).start()
    for i in range(blocks):
        for j in range(1, members):
            kv_x_copy(i, j).wait_recv()

    tokens = kseg_ref.shape[1]
    distance = (
        c * rows
        + lax.broadcasted_iota(jnp.int32, (rows, tokens), 0)
        - lax.broadcasted_iota(jnp.int32, (rows, tokens), 1)
    )
    allowed = (distance >= 0) & (distance < WIN) & (qseg_ref[...] == kseg_ref[...])
    keys_all = kv_all[...].reshape(tokens, 2 * HD)
    for head in range(cols // HD):
        span = slice(head * HD, (head + 1) * HD)
        scores = lax.dot_general(
            q_ref[:, span], keys_all[:, :HD], (((1,), (1,)), ((), ())), preferred_element_type=jnp.float32
        ) * (1.0 / math.sqrt(HD))
        scores = jnp.where(allowed, scores, -1e30)
        weights = jnp.exp(scores - jnp.max(scores, axis=-1, keepdims=True))
        probs = (weights / jnp.sum(weights, axis=-1, keepdims=True)).astype(jnp.bfloat16)
        att[c, :, span] = jnp.dot(probs, keys_all[:, HD:], preferred_element_type=jnp.float32).astype(jnp.bfloat16)
    relay(c, lambda copy: copy.start())

    tile = math.gcd(width, 256)

    def multiply(source, at, weight, target, i):
        @pl.loop(0, weight.shape[1] // tile)
        def _(n):
            span = pl.ds(pl.multiple_of(n * tile, tile), tile)
            target[i, :, span] = jnp.dot(
                source[at], weight[:, span], preferred_element_type=jnp.float32
            ).astype(jnp.bfloat16)

    @pl.loop(0, blocks + 2)
    def _(tick):
        @pl.when(tick < blocks)
        def _():
            b = block_at(tick)

            @pl.when(tick > 0)
            def _():
                att_right(b).wait_recv()
                relay(b, lambda copy: copy.start())

            multiply(att, b, ow_ref, heads, tick)
            for j in range(1, members):
                sum_copy(tick, j).start()

        @pl.when((tick > 0) & (tick < blocks + 1))
        def _():
            i = tick - 1
            b = block_at(i)
            sums[i, m] = heads[i, rows_of(m)]

            @pl.when(i > 0)
            def _():
                res_arrival(b).wait_recv()

            total = resid_in[b].astype(jnp.float32)
            for j in range(1, members):
                sum_copy(i, j).wait_recv()
            for j in range(members):
                total = total + sums[i, j].astype(jnp.float32)
            resid = total.astype(jnp.bfloat16)
            gained[i, rows_of(m)] = (resid.astype(jnp.float32) * gain_ref[...]).astype(jnp.bfloat16)
            for j in range(1, members):
                gain_copy(i, j).start()
            resid_in[b] = resid

            @pl.when(i > 0)
            def _():
                row_copy(b).start()

        @pl.when(tick > 1)
        def _():
            i = tick - 2
            for j in range(1, members):
                gain_copy(i, j).wait_recv()
            multiply(gained, i, lw_ref, partial, i)

            @pl.when(i > 0)
            def _():
                mix_copy(i, block_at(i)).start()

    resid_rows[c] = resid_in[c]
    for i in range(1, blocks):
        row_arrival(i).wait_recv()
    squares = jnp.zeros((piece, 1), jnp.float32)
    for k in range(blocks):
        resid = resid_rows[k]
        resid_ref[:, k * width : (k + 1) * width] = resid
        resid_f32 = resid.astype(jnp.float32)
        squares = squares + jnp.sum(resid_f32 * resid_f32, axis=-1, keepdims=True)
    inverse[m] = jnp.broadcast_to(lax.rsqrt(squares / (blocks * width) + 1e-06), inverse.shape[1:])
    for j in range(1, members):
        inv_copy(j).start()
    for i in range(1, blocks):
        mix_arrival(i).wait_recv()
    for j in range(1, members):
        inv_copy(j).wait_recv()
    scale = inverse[...].reshape(rows, inverse.shape[2])[:, 0:1]
    mixed[c] = partial[0]
    total = mixed[0].astype(jnp.float32)
    for k in range(1, blocks):
        total = total + mixed[k].astype(jnp.float32)
    ext[HALO:] = (total * scale).astype(jnp.bfloat16)
    rim_copy().start()
    rim_copy().wait()
    ext[:HALO] = rim[...]

    scan_kernel(ext, flags_ref, conv_ref, wd_ref, wi_ref, vec_ref, keep, state)

    ends[c, 0:8] = keep[rows - 8 :]
    ends[c, 8:16] = state[rows - 8 :]
    for i in range(1, blocks):
        end_copy(i).start()
    for i in range(1, blocks):
        end_copy(i).wait_recv()
    incoming = jnp.zeros((1, keep.shape[1]), jnp.float32)
    for source in range(blocks - 1):
        incoming = jnp.where(source < c, ends[source, 7:8] * incoming + ends[source, 15:16], incoming)
    lru_ref[...] = (state[...] + keep[...] * incoming).astype(jnp.bfloat16)

    for j in range(1, members):
        inv_copy(j).wait_send()
    for i in range(blocks):
        for j in range(1, members):
            kv_x_copy(i, j).wait_send()
            sum_copy(i, j).wait_send()
            gain_copy(i, j).wait_send()
        relay(block_at(i), lambda copy: copy.wait_send())
        if i:
            kv_z_copy(i).wait_send()
            res_copy(i).wait_send()
            row_copy(block_at(i)).wait_send()
            mix_copy(i, block_at(i)).wait_send()
            end_copy(i).wait_send()


def local_stationary(
    queries,
    keyvals,
    segment_ids,
    residual,
    out_weight,
    lru_weight,
    conv_weight,
    gate_decay_w,
    gate_input_w,
    gate_decay_b,
    gate_input_b,
    decay_codes,
    norm_gain,
):
    rows, cols = queries.shape
    blocks, members = lax.axis_size("ctx"), lax.axis_size("mp")
    piece = rows // members
    width, channels = out_weight.shape[1], lru_weight.shape[1]
    ctx_index = lax.axis_index("ctx")
    flags, vectors, query_seg = recurrence_inputs(rows, segment_ids, gate_decay_b, gate_input_b, decay_codes)
    gain = lax.dynamic_slice_in_dim(norm_gain, ctx_index * width, width)[None]
    bf16, f32 = jnp.bfloat16, jnp.float32
    vmem = pl.BlockSpec(memory_space=pltpu.VMEM)
    sems = [(blocks,), (blocks, members), (2 * blocks,), (blocks,), (blocks, members), (blocks, members)]
    sems = sems + [(blocks,), (blocks,), (members,), (1,), (blocks,)]
    return pl.pallas_call(
        functools.partial(fused_kernel, blocks, members),
        out_shape=(jax.ShapeDtypeStruct(residual.shape, bf16), jax.ShapeDtypeStruct((rows, channels), bf16)),
        in_specs=[vmem] * 13,
        out_specs=(vmem, vmem),
        scratch_shapes=[
            pltpu.VMEM((blocks * members,) + keyvals.shape, bf16),
            pltpu.VMEM((blocks, rows, cols), bf16),
            pltpu.VMEM((blocks, rows, width), bf16),
            pltpu.VMEM((blocks, members, piece, width), bf16),
            pltpu.VMEM((blocks, rows, width), bf16),
            pltpu.VMEM((blocks, rows, channels), bf16),
            pltpu.VMEM((blocks, rows, channels), bf16),
            pltpu.VMEM((blocks, piece, width), bf16),
            pltpu.VMEM((blocks, piece, width), bf16),
            pltpu.VMEM((members, piece, 128), f32),
            pltpu.VMEM((rows + HALO, channels), bf16),
            pltpu.VMEM((HALO, channels), bf16),
            pltpu.VMEM((blocks, 16, channels), f32),
            pltpu.VMEM((rows, channels), f32),
            pltpu.VMEM((rows, channels), f32),
        ]
        + [pltpu.SemaphoreType.DMA((2,) + shape) for shape in sems],
        compiler_params=pltpu.CompilerParams(
            collective_id=0, has_side_effects=True, vmem_limit_bytes=56 * 1024 * 1024
        ),
    )(
        queries, keyvals, query_seg[:, None], segment_ids[None], residual, out_weight, lru_weight, gain,
        flags, conv_weight, gate_decay_w, gate_input_w, vectors,
    )


def solution(mesh):
    in_specs = (
        P(("groups", "ctx"), "mp"),
        P(("groups", "ctx", "mp"), None),
        P("groups"),
        P(("groups", "ctx", "mp"), None),
        P("mp", "ctx"),
        P("ctx", "mp"),
        P(None, "mp"),
        P("mp", None, None),
        P("mp", None, None),
        P("mp"),
        P("mp"),
        P("mp"),
        P(),
    )
    out_specs = (P(("groups", "ctx", "mp"), None), P(("groups", "ctx"), "mp"))

    def body(*args):
        segment_ids, out_weight = args[2], args[4]
        stationary = segment_ids.shape[0] <= lax.axis_size("ctx") * out_weight.shape[1] // 2
        return (local_stationary if stationary else local)(*args)

    return jax.shard_map(body, mesh=mesh, in_specs=in_specs, out_specs=out_specs, check_vma=False)
```

```python
import functools
import math

import jax
import jax.numpy as jnp
from jax import lax
from jax.experimental import pallas as pl
from jax.experimental.pallas import tpu as pltpu
from jax.sharding import PartitionSpec as P

HD = 256
WIN = 2048
CONV = 4
LEVELS = 16
BW = 256


def shifted_2(value, axis, steps):
    count = lax.axis_size(axis)
    initial, last = (max(0, -steps), min(count, count - steps))
    return lax.ppermute(value, axis, [(source, source + steps) for source in range(initial, last)])


def decay_rates():
    levels = jnp.arange(LEVELS, dtype=jnp.float32)
    return 0.006 * jnp.exp(-levels * (math.log(3000.0) / (LEVELS - 1)))


def chain_link(former, latter):
    return (former[0] * latter[0], latter[0] * former[1] + latter[1])


def rms_scaled(values, norm_gain):
    value_f32 = values.astype(jnp.float32)
    inverse = lax.rsqrt(jnp.mean(value_f32 * value_f32, axis=-1, keepdims=True) + 1e-06)
    return (value_f32 * inverse * norm_gain).astype(jnp.bfloat16)


def attend_local(queries, keys_all, allowed):
    rows_here = queries.shape[0]
    heads_here = queries.shape[1] // HD
    query_heads = queries.reshape(rows_here, heads_here, HD)
    score_scale = 1.0 / math.sqrt(HD)
    scores = (
        jnp.einsum("thd,kd->htk", query_heads, keys_all[:, :HD], preferred_element_type=jnp.float32)
        * score_scale
    )
    scores = jnp.where(allowed[None], scores, -1e30)
    row_top = jnp.max(scores, axis=-1, keepdims=True)
    weights = jnp.exp(scores - row_top)
    probs = (weights / jnp.sum(weights, axis=-1, keepdims=True)).astype(jnp.bfloat16)
    gathered = jnp.einsum(
        "htk,kd->thd", probs, keys_all[:, HD:], preferred_element_type=jnp.float32
    )
    return gathered.reshape(rows_here, heads_here * HD).astype(jnp.bfloat16)


def local(
    queries,
    keyvals,
    segment_ids,
    residual,
    out_weight,
    lru_weight,
    conv_weight,
    gate_decay_w,
    gate_input_w,
    gate_decay_b,
    gate_input_b,
    decay_codes,
    norm_gain,
):
    rows_here = queries.shape[0]
    ctx_index = lax.axis_index("ctx")
    back_blocks = WIN // rows_here
    own_kv = lax.all_gather(keyvals, "mp", axis=0, tiled=True)
    earlier = []
    moving = own_kv
    for offset in range(back_blocks):
        moving = shifted_2(moving, "ctx", 1)
        earlier = [moving] + earlier
    keys_all = jnp.concatenate(earlier + [own_kv], axis=0)
    pad_seg = jnp.concatenate([jnp.full((WIN,), -1, jnp.int32), segment_ids])
    query_seg = lax.dynamic_slice_in_dim(segment_ids, ctx_index * rows_here, rows_here)
    key_seg = lax.dynamic_slice_in_dim(
        pad_seg, ctx_index * rows_here, (back_blocks + 1) * rows_here
    )
    query_pos = ctx_index * rows_here + jnp.arange(rows_here, dtype=jnp.int32)
    key_pos = (ctx_index - back_blocks) * rows_here + jnp.arange(
        (back_blocks + 1) * rows_here, dtype=jnp.int32
    )
    distance = query_pos[:, None] - key_pos[None, :]
    allowed = (distance >= 0) & (distance < WIN) & (query_seg[:, None] == key_seg[None, :])
    attended = attend_local(queries, keys_all, allowed)
    head_part = jnp.dot(
        attended,
        lax.all_gather(out_weight, "ctx", axis=1, tiled=True),
        preferred_element_type=jnp.float32,
    )
    summed = lax.psum_scatter(
        head_part.astype(jnp.bfloat16), "mp", scatter_dimension=0, tiled=True
    ).astype(jnp.float32)
    resid_out = (summed + residual.astype(jnp.float32)).astype(jnp.bfloat16)
    normed = lax.all_gather(rms_scaled(resid_out, norm_gain), "mp", axis=0, tiled=True)
    lru_in = jnp.dot(
        normed,
        lax.all_gather(lru_weight, "ctx", axis=0, tiled=True),
        preferred_element_type=jnp.float32,
    ).astype(jnp.bfloat16)
    return resid_out, recurrence(
        lru_in, segment_ids, conv_weight, gate_decay_w, gate_input_w,
        gate_decay_b, gate_input_b, decay_codes,
    )


HALO = 16


def scan_kernel(ext_ref, flags_ref, conv_ref, wd_ref, wi_ref, vec_ref, keep_ref, state_ref):
    rows = state_ref.shape[0]
    groups = rows // 8
    flags = flags_ref[...]
    row_in_group = lax.broadcasted_iota(jnp.int32, (groups, 8, BW), 1)
    for block in range(state_ref.shape[1] // BW):
        cols = slice(block * BW, (block + 1) * BW)
        ext = ext_ref[:, cols].astype(jnp.float32)
        acc = conv_ref[0:1, cols] * ext[HALO:]
        for lag in range(1, CONV):
            moved = pltpu.roll(ext, lag, 0)[HALO:]
            acc = acc + jnp.where(flags[:, lag : lag + 1] > 0.5, conv_ref[lag : lag + 1, cols] * moved, 0.0)
        conv_out = acc.astype(jnp.bfloat16)
        decay_gate = jax.nn.sigmoid(
            jnp.dot(conv_out, wd_ref[block], preferred_element_type=jnp.float32) + vec_ref[0:1, cols]
        )
        input_gate = jax.nn.sigmoid(
            jnp.dot(conv_out, wi_ref[block], preferred_element_type=jnp.float32) + vec_ref[1:2, cols]
        )
        log_decay = -8.0 * decay_gate * vec_ref[2:3, cols]
        restart = flags[:, 0:1] > 0.5
        keep = jnp.where(restart, 0.0, jnp.exp(log_decay))
        x = 2.0 * log_decay
        poly = 1.0 + x * (1.0 / 6.0)
        for order in (5.0, 4.0, 3.0, 2.0):
            poly = 1.0 + x * (1.0 / order) * poly
        scale = jnp.where(restart, 1.0, jnp.sqrt(-x * poly))
        state = scale * input_gate * conv_out.astype(jnp.float32)
        keep = keep.reshape(groups, 8, BW)
        state = state.reshape(groups, 8, BW)
        for shift in (1, 2, 4):
            inside = row_in_group >= shift
            before_state = jnp.where(inside, pltpu.roll(state, shift, 1), 0.0)
            before_keep = jnp.where(inside, pltpu.roll(keep, shift, 1), 1.0)
            state = state + keep * before_state
            keep = keep * before_keep
        keep_carry = jnp.ones((1, BW), jnp.float32)
        state_carry = jnp.zeros((1, BW), jnp.float32)
        for group in range(groups):
            rows_now = slice(group * 8, group * 8 + 8)
            state_now = state[group] + keep[group] * state_carry
            keep_now = keep[group] * keep_carry
            state_ref[rows_now, cols] = state_now
            keep_ref[rows_now, cols] = keep_now
            state_carry = state_now[7:8]
            keep_carry = keep_now[7:8]


def recurrence_inputs(rows_here, segment_ids, gate_decay_b, gate_input_b, decay_codes):
    ctx_index = lax.axis_index("ctx")
    pad_seg = jnp.concatenate([jnp.full((CONV - 1,), -1, jnp.int32), segment_ids])
    ext_seg = lax.dynamic_slice_in_dim(pad_seg, ctx_index * rows_here, rows_here + CONV - 1)
    query_seg = ext_seg[CONV - 1 :]
    lagged = [ext_seg[CONV - 1 - lag : CONV - 1 - lag + rows_here] == query_seg for lag in range(CONV)]
    flags = jnp.stack([~lagged[1]] + lagged[1:], axis=1).astype(jnp.float32)
    levels = jnp.arange(LEVELS, dtype=jnp.int32)
    decay_rate = jnp.sum(
        jnp.where(decay_codes[:, None] == levels[None, :], decay_rates()[None, :], 0.0), axis=1
    )
    vectors = jnp.stack([gate_decay_b, gate_input_b, decay_rate])
    return flags, vectors, query_seg


def recurrence(
    lru_in, segment_ids, conv_weight, gate_decay_w, gate_input_w, gate_decay_b, gate_input_b, decay_codes
):
    rows_here, channels = lru_in.shape
    ctx_index = lax.axis_index("ctx")
    rim_rows = shifted_2(lru_in[rows_here - HALO :], "ctx", 1)
    extended = jnp.concatenate([rim_rows, lru_in], axis=0)
    flags, vectors, _ = recurrence_inputs(rows_here, segment_ids, gate_decay_b, gate_input_b, decay_codes)
    full = jax.ShapeDtypeStruct((rows_here, channels), jnp.float32)
    cum_keep, local_state = pl.pallas_call(
        scan_kernel,
        out_shape=(full, full),
        compiler_params=pltpu.CompilerParams(vmem_limit_bytes=40 * 1024 * 1024),
    )(extended, flags, conv_weight, gate_decay_w, gate_input_w, vectors)
    ends = jnp.stack([cum_keep[rows_here - 1], local_state[rows_here - 1]])
    all_ends = lax.all_gather(ends, "ctx", axis=0)
    incoming = jnp.zeros((channels,), jnp.float32)
    for source in range(lax.axis_size("ctx") - 1):
        incoming = jnp.where(
            source < ctx_index, all_ends[source, 0] * incoming + all_ends[source, 1], incoming
        )
    states = local_state + cum_keep * incoming[None, :]
    return states.astype(jnp.bfloat16)


def fused_kernel(
    blocks, members, q_ref, kv_ref, qseg_ref, kseg_ref, res_ref, ow_ref, lw_ref, gain_ref, flags_ref,
    conv_ref, wd_ref, wi_ref, vec_ref, resid_ref, lru_ref,
    kv_all, att, heads, sums, gained, partial, mixed, resid_in, resid_rows, inverse, ext, rim, ends, keep, state,
    kv_z, kv_x, att_s, res_s, sum_s, gain_s, row_s, mix_s, inv_s, rim_s, end_s,
):
    group, c, m = lax.axis_index("groups"), lax.axis_index("ctx"), lax.axis_index("mp")
    rows, cols = q_ref.shape
    piece = rows // members
    width = ow_ref.shape[1]

    def ahead(offset):
        return lax.rem(c + offset, blocks)

    def behind(offset):
        return lax.rem(c + blocks - offset, blocks)

    def member(offset):
        return lax.rem(m + offset, members)

    def rows_of(which):
        return pl.ds(pl.multiple_of(which * piece, piece), piece)

    def cols_of(which):
        return pl.ds(pl.multiple_of(which * width, width), width)

    def send(src, dst, sems, index, to_c, to_m, landing=None):
        landing = index if landing is None else landing
        return pltpu.make_async_remote_copy(
            src_ref=src, dst_ref=dst, send_sem=sems.at[(0, *index)], recv_sem=sems.at[(1, *landing)],
            device_id=(group, to_c, to_m), device_id_type=pl.DeviceIdType.MESH,
        )

    def kv_z_copy(i):
        slot = kv_all.at[c * members + m]
        return send(kv_ref, slot, kv_z, (i,), ahead(i), m)

    def kv_x_copy(i, j):
        slot = kv_all.at[behind(i) * members + m]
        return send(slot, slot, kv_x, (i, j), c, member(j))

    def res_copy(i):
        return send(res_ref.at[:, cols_of(ahead(i))], resid_in.at[c], res_s, (i,), ahead(i), m, (c,))

    def res_arrival(b):
        return send(res_ref.at[:, cols_of(c)], resid_in.at[b], res_s, (0,), b, m, (b,))

    def att_right(b, span=slice(None)):
        return send(att.at[b, :, span], att.at[b, :, span], att_s, (b,), ahead(1), m)

    def att_left(b, span=slice(None)):
        return send(att.at[b, :, span], att.at[b, :, span], att_s, (b + blocks,), behind(1), m, (b,))

    def relay(b, act, span=slice(None)):
        @pl.when((b <= c) & (c < blocks - 1))
        def _():
            act(att_right(b, span))

        @pl.when((b >= c) & (c > 0))
        def _():
            act(att_left(b, span))

    nearer = jnp.minimum(c, blocks - 1 - c)

    def block_at(tick):
        both = tick <= 2 * nearer
        steps = jnp.where(both, lax.div(tick + 1, 2), tick - nearer)
        leftward = jnp.where(both, lax.rem(tick, 2) == 1, c > nearer)
        return jnp.where(leftward, c - steps, c + steps)

    def sum_copy(i, j):
        return send(heads.at[i, rows_of(member(j))], sums.at[i, m], sum_s, (i, j), c, member(j))

    def gain_copy(i, j):
        return send(gained.at[i, rows_of(m)], gained.at[i, rows_of(m)], gain_s, (i, j), c, member(j))

    def row_copy(b):
        return send(resid_in.at[b], resid_rows.at[c], row_s, (b,), b, m, (c,))

    def mix_copy(i, b):
        return send(partial.at[i], mixed.at[c], mix_s, (b,), b, m, (c,))

    def row_arrival(i):
        return send(resid_in.at[0], resid_rows.at[c], row_s, (0,), ahead(i), m, (ahead(i),))

    def mix_arrival(i):
        return send(partial.at[0], mixed.at[c], mix_s, (0,), ahead(i), m, (ahead(i),))

    def inv_copy(j):
        return send(inverse.at[m], inverse.at[m], inv_s, (j,), c, member(j))

    def rim_copy():
        return send(ext.at[pl.ds(rows, HALO)], rim, rim_s, (0,), ahead(1), m)

    def end_copy(i):
        return send(ends.at[c], ends.at[c], end_s, (i,), ahead(i), m)

    barrier = pltpu.get_barrier_semaphore()
    for i in range(blocks):
        for j in range(members):
            if i or j:
                pl.semaphore_signal(
                    barrier, inc=1, device_id=(group, ahead(i), member(j)), device_id_type=pl.DeviceIdType.MESH
                )
    pl.semaphore_wait(barrier, blocks * members - 1)

    kv_all[c * members + m] = kv_ref[...]
    for i in range(1, blocks):
        kv_z_copy(i).start()
    for j in range(1, members):
        kv_x_copy(0, j).start()
    for i in range(1, blocks):
        res_copy(i).start()
    resid_in[c] = res_ref[:, cols_of(c)]
    for i in range(1, blocks):
        kv_z_copy(i).wait_recv()
        for j in range(1, members):
            kv_x_copy(i, j).start()
    for i in range(blocks):
        for j in range(1, members):
            kv_x_copy(i, j).wait_recv()

    tokens = kseg_ref.shape[1]
    distance = (
        c * rows
        + lax.broadcasted_iota(jnp.int32, (rows, tokens), 0)
        - lax.broadcasted_iota(jnp.int32, (rows, tokens), 1)
    )
    allowed = (distance >= 0) & (distance < WIN) & (qseg_ref[...] == kseg_ref[...])
    keys_all = kv_all[...].reshape(tokens, 2 * HD)
    for head in range(cols // HD):
        span = slice(head * HD, (head + 1) * HD)
        scores = lax.dot_general(
            q_ref[:, span], keys_all[:, :HD], (((1,), (1,)), ((), ())), preferred_element_type=jnp.float32
        ) * (1.0 / math.sqrt(HD))
        scores = jnp.where(allowed, scores, -1e30)
        weights = jnp.exp(scores - jnp.max(scores, axis=-1, keepdims=True))
        probs = (weights / jnp.sum(weights, axis=-1, keepdims=True)).astype(jnp.bfloat16)
        att[c, :, span] = jnp.dot(probs, keys_all[:, HD:], preferred_element_type=jnp.float32).astype(jnp.bfloat16)
        relay(c, lambda copy: copy.start(), span)

    tile = math.gcd(width, 256)

    def multiply(source, at, weight, target, i):
        @pl.loop(0, weight.shape[1] // tile)
        def _(n):
            span = pl.ds(pl.multiple_of(n * tile, tile), tile)
            target[i, :, span] = jnp.dot(
                source[at], weight[:, span], preferred_element_type=jnp.float32
            ).astype(jnp.bfloat16)

    @pl.loop(0, blocks + 2)
    def _(tick):
        @pl.when(tick < blocks)
        def _():
            b = block_at(tick)

            @pl.when(tick > 0)
            def _():
                att_right(b).wait_recv()
                relay(b, lambda copy: copy.start())

            multiply(att, b, ow_ref, heads, tick)
            for j in range(1, members):
                sum_copy(tick, j).start()

        @pl.when((tick > 0) & (tick < blocks + 1))
        def _():
            i = tick - 1
            b = block_at(i)
            sums[i, m] = heads[i, rows_of(m)]

            @pl.when(i > 0)
            def _():
                res_arrival(b).wait_recv()

            total = resid_in[b].astype(jnp.float32)
            for j in range(1, members):
                sum_copy(i, j).wait_recv()
            for j in range(members):
                total = total + sums[i, j].astype(jnp.float32)
            resid = total.astype(jnp.bfloat16)
            gained[i, rows_of(m)] = (resid.astype(jnp.float32) * gain_ref[:, cols_of(c)]).astype(jnp.bfloat16)
            for j in range(1, members):
                gain_copy(i, j).start()
            resid_in[b] = resid

            @pl.when(i > 0)
            def _():
                row_copy(b).start()

        @pl.when(tick > 1)
        def _():
            i = tick - 2
            for j in range(1, members):
                gain_copy(i, j).wait_recv()
            multiply(gained, i, lw_ref, partial, i)

            @pl.when(i > 0)
            def _():
                mix_copy(i, block_at(i)).start()

    resid_rows[c] = resid_in[c]
    for i in range(1, blocks):
        row_arrival(i).wait_recv()
    squares = jnp.zeros((piece, 1), jnp.float32)
    for k in range(blocks):
        resid = resid_rows[k]
        resid_ref[:, k * width : (k + 1) * width] = resid
        resid_f32 = resid.astype(jnp.float32)
        squares = squares + jnp.sum(resid_f32 * resid_f32, axis=-1, keepdims=True)
    inverse[m] = jnp.broadcast_to(lax.rsqrt(squares / (blocks * width) + 1e-06), inverse.shape[1:])
    for j in range(1, members):
        inv_copy(j).start()
    for i in range(1, blocks):
        mix_arrival(i).wait_recv()
    for j in range(1, members):
        inv_copy(j).wait_recv()
    scale = inverse[...].reshape(rows, inverse.shape[2])[:, 0:1]
    mixed[c] = partial[0]
    total = mixed[0].astype(jnp.float32)
    for k in range(1, blocks):
        total = total + mixed[k].astype(jnp.float32)
    ext[HALO:] = (total * scale).astype(jnp.bfloat16)
    rim_copy().start()
    rim_copy().wait()
    ext[:HALO] = rim[...]

    scan_kernel(ext, flags_ref, conv_ref, wd_ref, wi_ref, vec_ref, keep, state)

    ends[c, 0:8] = keep[rows - 8 :]
    ends[c, 8:16] = state[rows - 8 :]
    for i in range(1, blocks):
        end_copy(i).start()
    for i in range(1, blocks):
        end_copy(i).wait_recv()
    incoming = jnp.zeros((1, keep.shape[1]), jnp.float32)
    for source in range(blocks - 1):
        incoming = jnp.where(source < c, ends[source, 7:8] * incoming + ends[source, 15:16], incoming)
    lru_ref[...] = (state[...] + keep[...] * incoming).astype(jnp.bfloat16)

    for j in range(1, members):
        inv_copy(j).wait_send()
    for i in range(blocks):
        for j in range(1, members):
            kv_x_copy(i, j).wait_send()
            sum_copy(i, j).wait_send()
            gain_copy(i, j).wait_send()
        relay(block_at(i), lambda copy: copy.wait_send())
        if i:
            kv_z_copy(i).wait_send()
            res_copy(i).wait_send()
            row_copy(block_at(i)).wait_send()
            mix_copy(i, block_at(i)).wait_send()
            end_copy(i).wait_send()


def local_stationary(
    queries,
    keyvals,
    segment_ids,
    residual,
    out_weight,
    lru_weight,
    conv_weight,
    gate_decay_w,
    gate_input_w,
    gate_decay_b,
    gate_input_b,
    decay_codes,
    norm_gain,
):
    rows, cols = queries.shape
    blocks, members = lax.axis_size("ctx"), lax.axis_size("mp")
    piece = rows // members
    width, channels = out_weight.shape[1], lru_weight.shape[1]
    ctx_index = lax.axis_index("ctx")
    flags, vectors, query_seg = recurrence_inputs(rows, segment_ids, gate_decay_b, gate_input_b, decay_codes)
    gain = norm_gain[None]
    bf16, f32 = jnp.bfloat16, jnp.float32
    vmem = pl.BlockSpec(memory_space=pltpu.VMEM)
    sems = [(blocks,), (blocks, members), (2 * blocks,), (blocks,), (blocks, members), (blocks, members)]
    sems = sems + [(blocks,), (blocks,), (members,), (1,), (blocks,)]
    return pl.pallas_call(
        functools.partial(fused_kernel, blocks, members),
        out_shape=(jax.ShapeDtypeStruct(residual.shape, bf16), jax.ShapeDtypeStruct((rows, channels), bf16)),
        in_specs=[vmem] * 13,
        out_specs=(vmem, vmem),
        scratch_shapes=[
            pltpu.VMEM((blocks * members,) + keyvals.shape, bf16),
            pltpu.VMEM((blocks, rows, cols), bf16),
            pltpu.VMEM((blocks, rows, width), bf16),
            pltpu.VMEM((blocks, members, piece, width), bf16),
            pltpu.VMEM((blocks, rows, width), bf16),
            pltpu.VMEM((blocks, rows, channels), bf16),
            pltpu.VMEM((blocks, rows, channels), bf16),
            pltpu.VMEM((blocks, piece, width), bf16),
            pltpu.VMEM((blocks, piece, width), bf16),
            pltpu.VMEM((members, piece, 128), f32),
            pltpu.VMEM((rows + HALO, channels), bf16),
            pltpu.VMEM((HALO, channels), bf16),
            pltpu.VMEM((blocks, 16, channels), f32),
            pltpu.VMEM((rows, channels), f32),
            pltpu.VMEM((rows, channels), f32),
        ]
        + [pltpu.SemaphoreType.DMA((2,) + shape) for shape in sems],
        compiler_params=pltpu.CompilerParams(
            collective_id=0, has_side_effects=True, vmem_limit_bytes=56 * 1024 * 1024
        ),
    )(
        queries, keyvals, query_seg[:, None], segment_ids[None], residual, out_weight, lru_weight, gain,
        flags, conv_weight, gate_decay_w, gate_input_w, vectors,
    )


def solution(mesh):
    in_specs = (
        P(("groups", "ctx"), "mp"),
        P(("groups", "ctx", "mp"), None),
        P("groups"),
        P(("groups", "ctx", "mp"), None),
        P("mp", "ctx"),
        P("ctx", "mp"),
        P(None, "mp"),
        P("mp", None, None),
        P("mp", None, None),
        P("mp"),
        P("mp"),
        P("mp"),
        P(),
    )
    out_specs = (P(("groups", "ctx", "mp"), None), P(("groups", "ctx"), "mp"))

    def body(*args):
        segment_ids, out_weight = args[2], args[4]
        stationary = segment_ids.shape[0] <= lax.axis_size("ctx") * out_weight.shape[1] // 2
        return (local_stationary if stationary else local)(*args)

    return jax.shard_map(body, mesh=mesh, in_specs=in_specs, out_specs=out_specs, check_vma=False)
```
